512 devices in a mesh: seq: 32 (over z_hi, x, core), head: 16 (over z_lo, y).
Axes of the slice: x: 4, y: 4, z: 16 (z_hi: 4, z_lo: 4; z = z_hi * 4 + z_lo), core: 2. Of those that a mesh axis runs over, the one named last changes fastest.
Arguments:
- query_rows: bfloat16 [4096, 2048], P('seq', 'head'), may hold values from -6 to 6
- key_rows: bfloat16 [4096, 128], P('seq'), may hold values from -6 to 6
- value_rows: bfloat16 [4096, 128], P('seq'), may hold values from -6 to 6
- out_grad: bfloat16 [4096, 2048], P('seq', 'head'), may hold values from -3 to 3
Outputs:
- attended: bfloat16 [4096, 2048], P('seq', 'head')
- query_grad: bfloat16 [4096, 2048], P('seq', 'head')
- key_grad: bfloat16 [4096, 128], P('seq')
- value_grad: bfloat16 [4096, 128], P('seq')
The draws below stay inside these ranges and needn't reach their ends.
All inputs are finite; a program needn't handle non-finite values.
Results may differ from the reference program's by a relative error of at most 0.023.
Values may be sent and summed in bfloat16 or wider, within the bound.
A program may use at most 64 MiB of HBM per device.

```python
import jax
import jax.numpy as jnp
import numpy as np
from jax import lax

D = 128
H = 16
TOK_DEV = 128
FEAT = 8256
TOKENS = 4096


def block_scale(own_key, extent, split, low, top_value):
    loudness, own = 1.0, jax.random.fold_in(own_key, 6)
    for position, blocks in split:
        draws = jnp.exp(jax.random.uniform(jax.random.fold_in(own, position), (blocks,), jnp.float32, low / len(split), top_value / len(split)))
        loudness = loudness * jnp.repeat(draws, extent[position] // blocks).reshape([-1 if axis == position else 1 for axis in range(len(extent))])
    return loudness


def bell_draw(stream_key, shape, deviation, limit, shards=(), kind=jnp.bfloat16):
    level = block_scale(stream_key, shape, shards, -0.22, 0.18) if shards else 1.0
    array = jax.random.normal(stream_key, shape, jnp.float32) * deviation * level
    return jnp.minimum(jnp.maximum(array, -limit), limit).astype(kind)


def setup_inputs(seed: int = 0) -> dict:
    streams_of = jax.random.split(jax.random.key(seed), 5)
    query_rows = bell_draw(streams_of[0], (TOKENS, H * D), 1.0, 6.0, ((0, 32), (1, 16)))
    key_rows = bell_draw(streams_of[1], (TOKENS, D), 1.0, 6.0, ((0, 32),))
    value_rows = bell_draw(streams_of[2], (TOKENS, D), 1.0, 6.0, ((0, 32),))
    out_grad = bell_draw(streams_of[3], (TOKENS, H * D), 0.5, 3.0, ((0, 32), (1, 16)))
    return {"query_rows": query_rows, "key_rows": key_rows, "value_rows": value_rows, "out_grad": out_grad}


EPSILON = 1e-06

def pair_tables(head_width):
    first_index, second_index = np.triu_indices(head_width)
    return (jnp.asarray(first_index, dtype=jnp.int32), jnp.asarray(second_index, dtype=jnp.int32))

def rounded(quantity):
    return lax.optimization_barrier(quantity.astype(jnp.bfloat16)).astype(jnp.float32)

def expand(source, first_index, second_index):
    return jnp.take(source, first_index, axis=-1) * jnp.take(source, second_index, axis=-1)

def spread_back(coeffs, source, first_index, second_index, head_width):
    left_terms = rounded(coeffs * jnp.take(source, second_index, axis=-1))
    right_terms = rounded(coeffs * jnp.take(source, first_index, axis=-1))
    summed = jax.ops.segment_sum(left_terms.T, first_index, num_segments=head_width)
    summed = summed + jax.ops.segment_sum(right_terms.T, second_index, num_segments=head_width)
    return summed.T

def reference(query_rows, key_rows, value_rows, out_grad):
    first_index, second_index = pair_tables(D)
    multiplicity = jnp.where(first_index == second_index, 1.0, 2.0).astype(jnp.float32)
    blocks = TOKENS // TOK_DEV
    query_blocks = query_rows.reshape(blocks, TOK_DEV, H, D).transpose(0, 2, 1, 3)
    grad_blocks = out_grad.reshape(blocks, TOK_DEV, H, D).transpose(0, 2, 1, 3)
    key_blocks = key_rows.reshape(blocks, TOK_DEV, D)
    value_blocks = value_rows.reshape(blocks, TOK_DEV, D)
    places = jnp.arange(TOK_DEV, dtype=jnp.int32)
    causal = places[:, None] >= places[None, :]

    def forward_block(running, inputs):
        query_block, grad_block, key_block, value_block = inputs
        prefix = rounded(running)
        key_float = key_block.astype(jnp.float32)
        value_float = value_block.astype(jnp.float32)

        def per_head(carried, head_pair):
            query_head, grad_head = head_pair
            query_float = query_head.astype(jnp.float32)
            products = jnp.dot(query_float, key_float.T, preferred_element_type=jnp.float32)
            weights = rounded(jnp.where(causal, products * products, 0.0))
            features = rounded(expand(query_float, first_index, second_index) * multiplicity)
            numerator = jnp.dot(weights, value_float, preferred_element_type=jnp.float32)
            numerator = numerator + jnp.dot(features, prefix, preferred_element_type=jnp.float32)
            root_mean = jnp.sqrt(lax.optimization_barrier(jnp.mean(numerator * numerator, axis=-1, keepdims=True)) + EPSILON)
            normed = numerator / root_mean
            grad_float = grad_head.astype(jnp.float32)
            numer_grad = rounded((grad_float - normed * lax.optimization_barrier(jnp.mean(grad_float * normed, axis=-1, keepdims=True))) / root_mean)
            value_dots = jnp.dot(numer_grad, value_float.T, preferred_element_type=jnp.float32)
            coefficient = rounded(jnp.where(causal, 2.0 * products * value_dots, 0.0))
            query_part = jnp.dot(numer_grad, prefix.T, preferred_element_type=jnp.float32) * multiplicity
            query_grad = jnp.dot(coefficient, key_float, preferred_element_type=jnp.float32)
            query_grad = query_grad + spread_back(query_part, query_float, first_index, second_index, D)
            dual_sum, key_sum, value_sum = carried
            dual_sum = dual_sum + jnp.dot(features.T, numer_grad, preferred_element_type=jnp.float32)
            key_sum = key_sum + jnp.dot(coefficient.T, query_float, preferred_element_type=jnp.float32)
            value_sum = value_sum + jnp.dot(weights.T, numer_grad, preferred_element_type=jnp.float32)
            return ((dual_sum, key_sum, value_sum), (normed.astype(jnp.bfloat16), query_grad.astype(jnp.bfloat16)))
        initial = (jnp.zeros((FEAT, D), jnp.float32), jnp.zeros((TOK_DEV, D), jnp.float32), jnp.zeros((TOK_DEV, D), jnp.float32))
        sums, outputs = lax.scan(per_head, initial, (query_block, grad_block))
        key_features = rounded(expand(key_float, first_index, second_index))
        running = running + jnp.dot(key_features.T, value_float, preferred_element_type=jnp.float32)
        return (running, (outputs[0], outputs[1], sums[0], sums[1], sums[2]))
    start_state = jnp.zeros((FEAT, D), jnp.float32)
    final_state, forward_out = lax.scan(forward_block, start_state, (query_blocks, grad_blocks, key_blocks, value_blocks))
    attended_blocks, query_grad_blocks, duals, key_sums, value_sums = forward_out

    def backward_block(running, inputs):
        dual_term, key_block, value_block, key_sum, value_sum = inputs
        suffix = rounded(running)
        key_float = key_block.astype(jnp.float32)
        value_float = value_block.astype(jnp.float32)
        key_features = rounded(expand(key_float, first_index, second_index))
        key_part = jnp.dot(value_float, suffix.T, preferred_element_type=jnp.float32)
        key_grad = key_sum + spread_back(key_part, key_float, first_index, second_index, D)
        value_grad = value_sum + jnp.dot(key_features, suffix, preferred_element_type=jnp.float32)
        return (running + dual_term, (key_grad.astype(jnp.bfloat16), value_grad.astype(jnp.bfloat16)))
    final_dual, backward_out = lax.scan(backward_block, start_state, (duals, key_blocks, value_blocks, key_sums, value_sums), reverse=True)
    attended = attended_blocks.transpose(0, 2, 1, 3).reshape(TOKENS, H * D)
    query_grad = query_grad_blocks.transpose(0, 2, 1, 3).reshape(TOKENS, H * D)
    key_grad = backward_out[0].reshape(TOKENS, D)
    value_grad = backward_out[1].reshape(TOKENS, D)
    return (attended, query_grad, key_grad, value_grad)
```

```python
import jax
import jax.numpy as jnp
from jax import lax
from jax.experimental import pallas as pl
from jax.experimental.pallas import tpu as pltpu
from jax.sharding import PartitionSpec as P

MESH = pl.DeviceIdType.MESH
EPSILON = 1e-06
BF = jnp.bfloat16
F32 = jnp.float32
ROWS = 128
D = 128
ORDER = (0, 1, 3, 2)
BACK = (2, 1, 3, 0)


def dot_last(a, b):
    return lax.dot_general(a, b, (((1,), (1,)), ((), ())), preferred_element_type=F32)


def dot_first(a, b):
    return lax.dot_general(a, b, (((0,), (0,)), ((), ())), preferred_element_type=F32)


def dot(a, b):
    return jnp.dot(a, b, preferred_element_type=F32)


def kernel(
    q_in, k_in, v_in, g_in,
    att_ref, dq_ref, dkv_ref,
    qall, ngall, gbuf, kv, s_ref, w_ref, part, parts, partr,
    dqacc, dqs, dqr, dkvs, yr, zs, zr, fin,
    lsem, zsem, zrsem, csem, qsem, qrsem, fsem, frsem,
    nsem, nrsem, gsem, grsem, dsem, drsem, ysem, yrsem, asem, arsem, osem, orsem,
):
    seq, head = lax.axis_index("seq"), lax.axis_index("head")
    zhi, x, core = seq // 8, (seq // 2) % 4, seq % 2
    zlo, y = head // 4, head % 4

    def dev(dzhi=0, dx=0, dcore=0, dzlo=0, dy=0):
        return (
            (((zhi + dzhi) % 4) * 4 + (x + dx) % 4) * 2 + (core + dcore) % 2,
            ((zlo + dzlo) % 4) * 4 + (y + dy) % 4,
        )

    peers = [dev(dx=e) for e in (1, 2, 3)]
    peers += [dev(dcore=r, dy=f) for r in (0, 1) for f in range(4) if (r, f) != (0, 0)]
    peers += [dev(dzhi=d, dzlo=m) for d in range(4) for m in range(4) if (d, m) != (0, 0)]
    peers += [dev(dy=f, dzlo=m) for f in (1, 2, 3) for m in (1, 2, 3)]
    barrier = pltpu.get_barrier_semaphore()
    for p in peers:
        pl.semaphore_signal(barrier, 1, device_id=p, device_id_type=MESH)
    loads = [
        pltpu.make_async_copy(k_in, kv.at[0, 0, 0], lsem.at[0]),
        pltpu.make_async_copy(v_in, kv.at[0, 0, 1], lsem.at[1]),
        pltpu.make_async_copy(q_in, qall.at[0], lsem.at[2]),
        pltpu.make_async_copy(g_in, gbuf, lsem.at[3]),
    ]
    for c in loads:
        c.start()
    for c in loads:
        c.wait()
    pl.semaphore_wait(barrier, len(peers))

    sent = []

    def send(src, dst, ssem, rsem, to):
        c = pltpu.make_async_remote_copy(
            src_ref=src, dst_ref=dst, send_sem=ssem, recv_sem=rsem, device_id=to, device_id_type=MESH
        )
        c.start()
        sent.append(c)
        return c

    mine = pl.ds(pl.multiple_of(y * 32, 32), 32)
    from_z = {}
    for d in (2, 1, 3):
        from_z[d] = send(
            kv.at[0, 0, :, mine, :], kv.at[d, 0, :, mine, :], zsem.at[d - 1], zrsem.at[d - 1], dev(dzhi=d)
        )
    from_core = send(kv.at[0, 0], kv.at[0, 1], csem.at[0], csem.at[1], dev(dcore=1))
    from_x = [
        send(qall.at[0], qall.at[4 - e], qsem.at[e - 1], qrsem.at[e - 1], dev(dx=e)) for e in (1, 2, 3)
    ]

    gap = lax.broadcasted_iota(jnp.int32, (ROWS, ROWS), 1) - lax.broadcasted_iota(
        jnp.int32, (ROWS, ROWS), 0
    )

    def forward(d):
        queries = qall[...].reshape(4 * ROWS, D)
        keys = kv[d, :, 0].reshape(2 * ROWS, D)
        values = kv[d, :, 1].reshape(2 * ROWS, D)
        products = dot_last(queries, keys)
        for e in range(4):
            block = (zhi * 4 + (x + e) % 4) * 2 + core
            for r in range(2):
                other = (((zhi + 4 - d) % 4) * 4 + x) * 2 + (core + r) % 2
                tile = products[e * ROWS : (e + 1) * ROWS, r * ROWS : (r + 1) * ROWS]
                tile = jnp.where(gap <= (block - other) * ROWS, tile, 0.0)
                s_ref[d, pl.ds(e * ROWS, ROWS), pl.ds(r * ROWS, ROWS)] = tile
                w_ref[d, pl.ds(e * ROWS, ROWS), pl.ds(r * ROWS, ROWS)] = (tile * tile).astype(BF)
        return dot(w_ref[d], values)

    from_core.wait_recv()
    for c in from_x:
        c.wait_recv()
    part[...] = forward(0)
    from_y = {}
    for d in ORDER[1:]:
        from_z[d].wait_recv()
        from_y[d] = []
        for r in (0, 1):
            for f in range(4):
                if (r, f) != (0, 0):
                    from_y[d].append(
                        send(
                            kv.at[d, 0, :, mine, :], kv.at[d, r, :, mine, :],
                            fsem.at[d - 1, r * 4 + f], frsem.at[d - 1, r * 4 + f], dev(dcore=r, dy=f),
                        )
                    )
    for d in ORDER[1:]:
        for c in from_y[d]:
            c.wait_recv()
        part[...] += forward(d)

    arrivals = []
    for e in (2, 1, 3):
        parts[e - 1] = part[pl.ds(e * ROWS, ROWS), :].astype(BF)
        arrivals.append(send(parts.at[e - 1], partr.at[e - 1], nsem.at[e - 1], nrsem.at[e - 1], dev(dx=e)))
    for c in arrivals:
        c.wait_recv()
    numerator = part[pl.ds(0, ROWS), :]
    for e in range(3):
        numerator = numerator + partr[e].astype(F32)
    root_mean = jnp.sqrt(jnp.mean(numerator * numerator, axis=-1, keepdims=True) + EPSILON)
    normed = numerator / root_mean
    grad = gbuf[...].astype(F32)
    ngall[0] = ((grad - normed * jnp.mean(grad * normed, axis=-1, keepdims=True)) / root_mean).astype(BF)
    from_x = [
        send(ngall.at[0], ngall.at[4 - e], gsem.at[e - 1], grsem.at[e - 1], dev(dx=e)) for e in (2, 1, 3)
    ]
    att_ref[...] = normed.astype(BF)
    for c in from_x:
        c.wait_recv()

    queries = qall[...].reshape(4 * ROWS, D)
    grads = ngall[...].reshape(4 * ROWS, D)
    dqacc[...] = jnp.zeros_like(dqacc)
    from_y = {}
    for d in BACK:
        keys = kv[d, :, 0].reshape(2 * ROWS, D)
        values = kv[d, :, 1].reshape(2 * ROWS, D)
        coefficient = (2.0 * s_ref[d] * dot_last(grads, values)).astype(BF)
        dkvs[d, :, 0] = dot_first(coefficient, queries).astype(BF).reshape(2, ROWS, D)
        dkvs[d, :, 1] = dot_first(w_ref[d], grads).astype(BF).reshape(2, ROWS, D)
        from_y[d] = []
        for r in (0, 1):
            for f in range(4):
                if (r, f) != (0, 0):
                    rows = pl.ds(pl.multiple_of(((y + f) % 4) * 32, 32), 32)
                    from_y[d].append(
                        send(
                            dkvs.at[d, r, :, rows, :], yr.at[d, r * 4 + f],
                            ysem.at[d, r * 4 + f], yrsem.at[d, r * 4 + f], dev(dcore=r, dy=f),
                        )
                    )
        dqacc[...] += dot(coefficient, keys)
    arrivals = []
    for e in (1, 2, 3):
        dqs[e - 1] = dqacc[pl.ds(e * ROWS, ROWS), :].astype(BF)
        arrivals.append(send(dqs.at[e - 1], dqr.at[e - 1], dsem.at[e - 1], drsem.at[e - 1], dev(dx=e)))

    from_z = []
    for d in BACK:
        for c in from_y[d]:
            c.wait_recv()
        total = dkvs[d, 0, :, mine, :].astype(F32)
        for i in range(1, 8):
            total = total + yr[d, i].astype(F32)
        zs[d] = total.astype(BF).reshape(4, 16, D)
        for m in range(4):
            if (d, m) != (0, 0):
                from_z.append(
                    send(
                        zs.at[d, (zlo + m) % 4], zr.at[d * 4 + m],
                        asem.at[d * 4 + m], arsem.at[d * 4 + m], dev(dzhi=4 - d, dzlo=m),
                    )
                )
    for c in arrivals:
        c.wait_recv()
    query_grad = dqacc[pl.ds(0, ROWS), :]
    for e in range(3):
        query_grad = query_grad + dqr[e].astype(F32)
    dq_ref[...] = query_grad.astype(BF)
    for c in from_z:
        c.wait_recv()
    total = zs[0, zlo].astype(F32)
    for i in range(1, 16):
        total = total + zr[i].astype(F32)
    place = pl.ds(pl.multiple_of(y * 32 + (zlo % 2) * 16, 16), 16)
    fin[...] = total.astype(BF)
    dkv_ref[zlo // 2, place, :] = total.astype(BF)
    last = []
    for f in range(4):
        for m in range(4):
            if (f, m) != (0, 0):
                last.append(
                    send(
                        fin, dkv_ref.at[zlo // 2, place, :],
                        osem.at[f * 4 + m], orsem.at[f * 4 + m], dev(dy=f, dzlo=m),
                    )
                )
    for c in last:
        c.wait_recv()
    for c in sent:
        c.wait_send()


def local(query_rows, key_rows, value_rows, out_grad):
    dma = pltpu.SemaphoreType.DMA
    vmem = pl.BlockSpec(memory_space=pltpu.VMEM)
    attended, query_grad, kv_grad = pl.pallas_call(
        kernel,
        out_shape=(
            jax.ShapeDtypeStruct((ROWS, D), BF),
            jax.ShapeDtypeStruct((ROWS, D), BF),
            jax.ShapeDtypeStruct((2, ROWS, D), BF),
        ),
        in_specs=[pl.BlockSpec(memory_space=pl.ANY)] * 4,
        out_specs=(vmem, vmem, vmem),
        scratch_shapes=[
            pltpu.VMEM((4, ROWS, D), BF),
            pltpu.VMEM((4, ROWS, D), BF),
            pltpu.VMEM((ROWS, D), BF),
            pltpu.VMEM((4, 2, 2, ROWS, D), BF),
            pltpu.VMEM((4, 4 * ROWS, 2 * ROWS), F32),
            pltpu.VMEM((4, 4 * ROWS, 2 * ROWS), BF),
            pltpu.VMEM((4 * ROWS, D), F32),
            pltpu.VMEM((3, ROWS, D), BF),
            pltpu.VMEM((3, ROWS, D), BF),
            pltpu.VMEM((4 * ROWS, D), F32),
            pltpu.VMEM((3, ROWS, D), BF),
            pltpu.VMEM((3, ROWS, D), BF),
            pltpu.VMEM((4, 2, 2, ROWS, D), BF),
            pltpu.VMEM((4, 8, 2, 32, D), BF),
            pltpu.VMEM((4, 4, 16, D), BF),
            pltpu.VMEM((16, 16, D), BF),
            pltpu.VMEM((16, D), BF),
            dma((4,)), dma((3,)), dma((3,)), dma((2,)), dma((3,)), dma((3,)), dma((3, 8)), dma((3, 8)),
            dma((3,)), dma((3,)), dma((3,)), dma((3,)), dma((3,)), dma((3,)),
            dma((4, 8)), dma((4, 8)), dma((16,)), dma((16,)), dma((16,)), dma((16,)),
        ],
        compiler_params=pltpu.CompilerParams(
            collective_id=0, has_side_effects=True, vmem_limit_bytes=48 * 2**20
        ),
    )(query_rows, key_rows, value_rows, out_grad)
    return attended, query_grad, kv_grad[0], kv_grad[1]


def solution(mesh):
    return jax.shard_map(
        local,
        mesh=mesh,
        in_specs=(P("seq", "head"), P("seq", None), P("seq", None), P("seq", "head")),
        out_specs=(P("seq", "head"), P("seq", "head"), P("seq", None), P("seq", None)),
        check_vma=False,
    )
```

```python
import jax
import jax.numpy as jnp
from jax import lax
from jax.experimental import pallas as pl
from jax.experimental.pallas import tpu as pltpu
from jax.sharding import PartitionSpec as P

MESH = pl.DeviceIdType.MESH
EPSILON = 1e-06
BF = jnp.bfloat16
F32 = jnp.float32
ROWS = 128
D = 128
BACK = (2, 1, 3, 0)


def dot_last(a, b):
    return lax.dot_general(a, b, (((1,), (1,)), ((), ())), preferred_element_type=F32)


def dot_first(a, b):
    return lax.dot_general(a, b, (((0,), (0,)), ((), ())), preferred_element_type=F32)


def dot(a, b):
    return jnp.dot(a, b, preferred_element_type=F32)


def kernel(
    in_ref,
    out_ref,
    qall, ngall, gbuf, kv, s_ref, w_ref, part, parts, partr,
    dqacc, dqs, dqr, dkvs, cr, ys, yr, zs, zr, fin,
    lsem, zsem, zrsem, csem, qsem, qrsem, fsem, frsem, psem, prsem,
    nsem, nrsem, gsem, grsem, dsem, drsem, ysem, yrsem, asem, arsem, osem, orsem,
):
    seq, head = lax.axis_index("seq"), lax.axis_index("head")
    zhi, x, core = seq // 8, (seq // 2) % 4, seq % 2
    zlo, y = head // 4, head % 4

    def dev(dzhi=0, dx=0, dcore=0, dzlo=0, dy=0):
        return (
            (((zhi + dzhi) % 4) * 4 + (x + dx) % 4) * 2 + (core + dcore) % 2,
            ((zlo + dzlo) % 4) * 4 + (y + dy) % 4,
        )

    has = {d: zhi >= d for d in range(4)}
    feeds = {d: zhi + d <= 3 for d in range(4)}

    peers = [dev(dzhi=d, dzlo=m) for d in (2, 1, 3, 0) for m in range(4) if (d, m) != (0, 0)]
    peers += [dev(dy=f, dzlo=m) for f in (1, 2, 3) for m in (1, 2, 3)]
    peers += [dev(dx=e) for e in (1, 2, 3)]
    peers += [dev(dy=f) for f in (1, 2, 3)] + [dev(dcore=1)]
    zr[...] = jnp.zeros_like(zr)
    barrier = pltpu.get_barrier_semaphore()
    for p in peers:
        pl.semaphore_signal(barrier, 1, device_id=p, device_id_type=MESH)
    loads = [
        pltpu.make_async_copy(in_ref.at[1], kv.at[0, 0, 0], lsem.at[0]),
        pltpu.make_async_copy(in_ref.at[2], kv.at[0, 0, 1], lsem.at[1]),
        pltpu.make_async_copy(in_ref.at[0], qall.at[0], lsem.at[2]),
        pltpu.make_async_copy(in_ref.at[3], gbuf, lsem.at[3]),
    ]
    for c in loads:
        c.start()
    for c in loads:
        c.wait()
    pl.semaphore_wait(barrier, len(peers))

    sent = []

    def make(src, dst, ssem, rsem, to, only=None):
        c = pltpu.make_async_remote_copy(
            src_ref=src, dst_ref=dst, send_sem=ssem, recv_sem=rsem, device_id=to, device_id_type=MESH
        )
        sent.append((c, only))
        return c

    def started(c):
        c.start()
        return c

    mine = pl.ds(pl.multiple_of(y * 32, 32), 32)
    from_z = {}
    for d in (1, 2, 3):
        from_z[d] = [
            make(
                kv.at[0, 0, :, mine, :], kv.at[d, 0, :, mine, :],
                zsem.at[d - 1], zrsem.at[d - 1], dev(dzhi=d), feeds[d],
            )
        ]
    for d in (2, 3, 1):

        @pl.when(feeds[d])
        def _():
            for c in from_z[d]:
                c.start()

    from_core = started(make(kv.at[0, 0], kv.at[0, 1], csem.at[0], csem.at[1], dev(dcore=1)))
    from_x = [
        started(make(qall.at[0], qall.at[4 - e], qsem.at[e - 1], qrsem.at[e - 1], dev(dx=e)))
        for e in (2, 1, 3)
    ]

    gap = lax.broadcasted_iota(jnp.int32, (ROWS, ROWS), 1) - lax.broadcasted_iota(
        jnp.int32, (ROWS, ROWS), 0
    )

    def forward(d):
        queries = qall[...].reshape(4 * ROWS, D)
        keys = kv[d, :, 0].reshape(2 * ROWS, D)
        values = kv[d, :, 1].reshape(2 * ROWS, D)
        products = dot_last(queries, keys)
        for e in range(4):
            block = (zhi * 4 + (x + e) % 4) * 2 + core
            for r in range(2):
                other = (((zhi + 4 - d) % 4) * 4 + x) * 2 + (core + r) % 2
                tile = products[e * ROWS : (e + 1) * ROWS, r * ROWS : (r + 1) * ROWS]
                if d == 0:
                    tile = jnp.where(gap <= (block - other) * ROWS, tile, 0.0)
                s_ref[d, pl.ds(e * ROWS, ROWS), pl.ds(r * ROWS, ROWS)] = tile
                w_ref[d, pl.ds(e * ROWS, ROWS), pl.ds(r * ROWS, ROWS)] = (tile * tile).astype(BF)
        return dot(w_ref[d], values)

    passed, from_y = {}, {}
    for d in (1, 2, 3):
        passed[d] = make(
            kv.at[d, 0], kv.at[d, 1], psem.at[d - 1], prsem.at[d - 1], dev(dcore=1), has[d]
        )
    for d in (1, 2, 3):
        from_y[d] = [
            make(
                kv.at[d, 0, :, mine, :], kv.at[d, 0, :, mine, :],
                fsem.at[d - 1, f], frsem.at[d - 1, f], dev(dy=f), has[d],
            )
            for f in (2, 1, 3)
        ]

    from_core.wait_recv()
    for c in from_x:
        c.wait_recv()
    part[...] = forward(0)
    for d in (1, 3, 2):

        @pl.when(has[d])
        def _():
            from_z[d][0].wait_recv()
            for c in from_y[d]:
                c.start()

    def hand_on(d, arriving):
        @pl.when(has[d])
        def _():
            for c in arriving:
                c.wait_recv()
            passed[d].start()

    def use(d):
        @pl.when(has[d])
        def _():
            passed[d].wait_recv()
            part[...] += forward(d)

    hand_on(1, from_y[1])
    hand_on(3, from_y[3])
    use(1)
    hand_on(2, from_y[2])
    use(3)
    use(2)

    arrivals = []
    for e in (2, 1, 3):
        parts[e - 1] = part[pl.ds(e * ROWS, ROWS), :].astype(BF)
        arrivals.append(
            started(make(parts.at[e - 1], partr.at[e - 1], nsem.at[e - 1], nrsem.at[e - 1], dev(dx=e)))
        )
    for c in arrivals:
        c.wait_recv()
    numerator = part[pl.ds(0, ROWS), :]
    for e in range(3):
        numerator = numerator + partr[e].astype(F32)
    root_mean = jnp.sqrt(jnp.mean(numerator * numerator, axis=-1, keepdims=True) + EPSILON)
    normed = numerator / root_mean
    grad = gbuf[...].astype(F32)
    ngall[0] = ((grad - normed * jnp.mean(grad * normed, axis=-1, keepdims=True)) / root_mean).astype(BF)
    from_x = [
        started(make(ngall.at[0], ngall.at[4 - e], gsem.at[e - 1], grsem.at[e - 1], dev(dx=e)))
        for e in (2, 1, 3)
    ]
    out_ref[0] = normed.astype(BF)
    for c in from_x:
        c.wait_recv()

    passed, from_y = {}, {}
    for d in range(4):
        passed[d] = make(dkvs.at[d, 1], cr.at[d], ysem.at[d, 0], yrsem.at[d, 0], dev(dcore=1), has[d])
        from_y[d] = []
        for f in (2, 1, 3):
            rows = pl.ds(pl.multiple_of(((y + f) % 4) * 32, 32), 32)
            from_y[d].append(
                make(ys.at[d, :, rows, :], yr.at[d, f], ysem.at[d, f], yrsem.at[d, f], dev(dy=f), has[d])
            )

    def backward(d):
        @pl.when(has[d])
        def _():
            queries = qall[...].reshape(4 * ROWS, D)
            grads = ngall[...].reshape(4 * ROWS, D)
            keys = kv[d, :, 0].reshape(2 * ROWS, D)
            values = kv[d, :, 1].reshape(2 * ROWS, D)
            coefficient = (2.0 * s_ref[d] * dot_last(grads, values)).astype(BF)
            dkvs[d, :, 0] = dot_first(coefficient, queries).astype(BF).reshape(2, ROWS, D)
            dkvs[d, :, 1] = dot_first(w_ref[d], grads).astype(BF).reshape(2, ROWS, D)
            passed[d].start()
            dqacc[...] += dot(coefficient, keys)

    def over_y(d):
        @pl.when(has[d])
        def _():
            passed[d].wait_recv()
            ys[d] = (dkvs[d, 0].astype(F32) + cr[d].astype(F32)).astype(BF)
            for c in from_y[d]:
                c.start()

    dqacc[...] = jnp.zeros_like(dqacc)
    late = []
    for d in BACK:
        backward(d)
        late.append(d)
        if len(late) > 2:
            over_y(late.pop(0))
    for d in late:
        over_y(d)
    arrivals = []
    for e in (2, 1, 3):
        dqs[e - 1] = dqacc[pl.ds(e * ROWS, ROWS), :].astype(BF)
        arrivals.append(
            started(make(dqs.at[e - 1], dqr.at[e - 1], dsem.at[e - 1], drsem.at[e - 1], dev(dx=e)))
        )

    from_z = {}
    for d in BACK:
        from_z[d] = []
        for m in (3, 2, 1, 0):
            if (d, m) != (0, 0):
                from_z[d].append(
                    make(
                        zs.at[d, (zlo + m) % 4], zr.at[d * 4 + m],
                        asem.at[d * 4 + m], arsem.at[d * 4 + m], dev(dzhi=4 - d, dzlo=m), has[d],
                    )
                )

        @pl.when(has[d])
        def _():
            for c in from_y[d]:
                c.wait_recv()
            total = ys[d, :, mine, :].astype(F32)
            for i in range(1, 4):
                total = total + yr[d, i].astype(F32)
            zs[d] = total.astype(BF).reshape(4, 16, D)
            for c in from_z[d]:
                c.start()

    for c in arrivals:
        c.wait_recv()
    query_grad = dqacc[pl.ds(0, ROWS), :]
    for e in range(3):
        query_grad = query_grad + dqr[e].astype(F32)
    out_ref[1] = query_grad.astype(BF)
    for d in (0, 1, 3, 2):

        @pl.when(feeds[d])
        def _():
            for c in from_z[d]:
                c.wait_recv()

    total = zs[0, zlo].astype(F32)
    for i in range(1, 16):
        total = total + zr[i].astype(F32)
    place = pl.ds(pl.multiple_of(y * 32 + (zlo % 2) * 16, 16), 16)
    fin[...] = total.astype(BF)
    out_ref[2 + zlo // 2, place, :] = total.astype(BF)
    last = []
    for f in (2, 1, 3, 0):
        for m in (3, 2, 1, 0):
            if (f, m) != (0, 0):
                last.append(
                    started(
                        make(
                            fin, out_ref.at[2 + zlo // 2, place, :],
                            osem.at[f * 4 + m], orsem.at[f * 4 + m], dev(dy=f, dzlo=m),
                        )
                    )
                )
    for c in last:
        c.wait_recv()
    for c, only in sent:
        if only is None:
            c.wait_send()
    for only in (*feeds.values(), *has.values()):

        @pl.when(only)
        def _():
            for c, o in sent:
                if o is only:
                    c.wait_send()


def local(query_rows, key_rows, value_rows, out_grad):
    dma = pltpu.SemaphoreType.DMA
    packed = pl.pallas_call(
        kernel,
        out_shape=jax.ShapeDtypeStruct((4, ROWS, D), BF),
        in_specs=[pl.BlockSpec(memory_space=pltpu.VMEM)],
        out_specs=pl.BlockSpec(memory_space=pltpu.VMEM),
        scratch_shapes=[
            pltpu.VMEM((4, ROWS, D), BF),
            pltpu.VMEM((4, ROWS, D), BF),
            pltpu.VMEM((ROWS, D), BF),
            pltpu.VMEM((4, 2, 2, ROWS, D), BF),
            pltpu.VMEM((4, 4 * ROWS, 2 * ROWS), F32),
            pltpu.VMEM((4, 4 * ROWS, 2 * ROWS), BF),
            pltpu.VMEM((4 * ROWS, D), F32),
            pltpu.VMEM((3, ROWS, D), BF),
            pltpu.VMEM((3, ROWS, D), BF),
            pltpu.VMEM((4 * ROWS, D), F32),
            pltpu.VMEM((3, ROWS, D), BF),
            pltpu.VMEM((3, ROWS, D), BF),
            pltpu.VMEM((4, 2, 2, ROWS, D), BF),
            pltpu.VMEM((4, 2, ROWS, D), BF),
            pltpu.VMEM((4, 2, ROWS, D), BF),
            pltpu.VMEM((4, 4, 2, 32, D), BF),
            pltpu.VMEM((4, 4, 16, D), BF),
            pltpu.VMEM((16, 16, D), BF),
            pltpu.VMEM((16, D), BF),
            dma((4,)), dma((3,)), dma((3,)), dma((2,)), dma((3,)), dma((3,)), dma((3, 4)), dma((3, 4)), dma((3,)), dma((3,)),
            dma((3,)), dma((3,)), dma((3,)), dma((3,)), dma((3,)), dma((3,)),
            dma((4, 4)), dma((4, 4)), dma((16,)), dma((16,)), dma((16,)), dma((16,)),
        ],
        compiler_params=pltpu.CompilerParams(
            collective_id=0, has_side_effects=True, vmem_limit_bytes=48 * 2**20
        ),
    )(jnp.stack((query_rows, key_rows, value_rows, out_grad)))
    return packed[0], packed[1], packed[2], packed[3]


def solution(mesh):
    return jax.shard_map(
        local,
        mesh=mesh,
        in_specs=(P("seq", "head"), P("seq", None), P("seq", None), P("seq", "head")),
        out_specs=(P("seq", "head"), P("seq", "head"), P("seq", None), P("seq", None)),
        check_vma=False,
    )
```

```python
import functools

import jax
import jax.numpy as jnp
from jax import lax
from jax.experimental import pallas as pl
from jax.experimental.pallas import tpu as pltpu
from jax.sharding import PartitionSpec as P

MESH = pl.DeviceIdType.MESH
EPSILON = 1e-06
BF = jnp.bfloat16
F32 = jnp.float32
ROWS = 128
D = 128
BACK = (2, 3, 1, 0)


def dot_last(a, b):
    return lax.dot_general(a, b, (((1,), (1,)), ((), ())), preferred_element_type=F32)


def dot_first(a, b):
    return lax.dot_general(a, b, (((0,), (0,)), ((), ())), preferred_element_type=F32)


def dot(a, b):
    return jnp.dot(a, b, preferred_element_type=F32)


def kernel(
    in_ref,
    out_ref,
    qall, ngall, gbuf, kv, s_ref, w_ref, part, parts, partr,
    dqacc, dqs, dqr, dkvs, cr, ys, yr, zs, zr, fin,
    lsem, zsem, zrsem, csem, qsem, qrsem, fsem, frsem, psem, prsem,
    nsem, nrsem, gsem, grsem, dsem, drsem, ysem, yrsem, asem, arsem, osem, orsem,
):
    seq, head = lax.axis_index("seq"), lax.axis_index("head")
    zhi, x, core = seq // 8, (seq // 2) % 4, seq % 2
    zlo, y = head // 4, head % 4

    def dev(dzhi=0, dx=0, dcore=0, dzlo=0, dy=0):
        return (
            (((zhi + dzhi) % 4) * 4 + (x + dx) % 4) * 2 + (core + dcore) % 2,
            ((zlo + dzlo) % 4) * 4 + (y + dy) % 4,
        )

    has = {d: zhi >= d for d in range(4)}
    feeds = {d: zhi + d <= 3 for d in range(4)}

    near = [dev(dzlo=m) for m in (1, 2, 3)]
    near += [dev(dy=f, dzlo=m) for f in (1, 2, 3) for m in (1, 2, 3)]
    near += [dev(dx=e) for e in (1, 2, 3)]
    near += [dev(dcore=r, dy=f) for r in (0, 1) for f in range(4) if (r, f) != (0, 0)]
    zr[...] = jnp.zeros_like(zr)
    barrier = pltpu.get_barrier_semaphore()
    owner = zlo < 2
    for d in (2, 3, 1):

        @pl.when(has[d])
        def _():
            pl.semaphore_signal(barrier, 1, device_id=dev(dzhi=4 - d), device_id_type=MESH)

    for d in (1, 2, 3):

        @pl.when(jnp.logical_and(feeds[d], owner))
        def _():
            for m in range(4):
                pl.semaphore_signal(barrier, 1, device_id=dev(dzhi=d, dzlo=m), device_id_type=MESH)

    for p in near:
        pl.semaphore_signal(barrier, 1, device_id=p, device_id_type=MESH)
    loads = [
        pltpu.make_async_copy(in_ref.at[1], kv.at[0, 0, 0], lsem.at[0]),
        pltpu.make_async_copy(in_ref.at[2], kv.at[0, 0, 1], lsem.at[1]),
        pltpu.make_async_copy(in_ref.at[0], qall.at[0], lsem.at[2]),
        pltpu.make_async_copy(in_ref.at[3], gbuf, lsem.at[3]),
    ]
    for c in loads:
        c.start()
    for c in loads:
        c.wait()
    pl.semaphore_wait(barrier, len(near) + (3 - zhi) + 2 * zhi)

    sent = []

    def make(src, dst, ssem, rsem, to, only=None):
        c = pltpu.make_async_remote_copy(
            src_ref=src, dst_ref=dst, send_sem=ssem, recv_sem=rsem, device_id=to, device_id_type=MESH
        )
        sent.append((c, only))
        return c

    def started(c):
        c.start()
        return c

    mine = pl.ds(pl.multiple_of(y * 32, 32), 32)
    from_z = {}
    for d in (1, 2, 3):
        from_z[d] = [
            make(
                kv.at[0, 0, :, mine, :], kv.at[d, 0, :, mine, :],
                zsem.at[d - 1], zrsem.at[d - 1], dev(dzhi=d), feeds[d],
            )
        ]
    for d in (2, 3, 1):

        @pl.when(feeds[d])
        def _():
            for c in from_z[d]:
                c.start()

    from_core = started(make(kv.at[0, 0], kv.at[0, 1], csem.at[0], csem.at[1], dev(dcore=1)))
    from_x = [
        started(make(qall.at[0], qall.at[4 - e], qsem.at[e - 1], qrsem.at[e - 1], dev(dx=e)))
        for e in (2, 1, 3)
    ]

    gap = lax.broadcasted_iota(jnp.int32, (ROWS, ROWS), 1) - lax.broadcasted_iota(
        jnp.int32, (ROWS, ROWS), 0
    )

    def forward(d):
        queries = qall[...].reshape(4 * ROWS, D)
        keys = kv[d, :, 0].reshape(2 * ROWS, D)
        values = kv[d, :, 1].reshape(2 * ROWS, D)
        products = dot_last(queries, keys)
        for e in range(4):
            block = (zhi * 4 + (x + e) % 4) * 2 + core
            for r in range(2):
                other = (((zhi + 4 - d) % 4) * 4 + x) * 2 + (core + r) % 2
                tile = products[e * ROWS : (e + 1) * ROWS, r * ROWS : (r + 1) * ROWS]
                if d == 0:
                    tile = jnp.where(gap <= (block - other) * ROWS, tile, 0.0)
                s_ref[d, pl.ds(e * ROWS, ROWS), pl.ds(r * ROWS, ROWS)] = tile
                w_ref[d, pl.ds(e * ROWS, ROWS), pl.ds(r * ROWS, ROWS)] = (tile * tile).astype(BF)
        return dot(w_ref[d], values)

    passed, from_y = {}, {}
    for d in (1, 3):
        passed[d] = make(
            kv.at[d, 0], kv.at[d, 1], csem.at[d + 1], csem.at[d + 2], dev(dcore=1), has[d]
        )
    for d in (1, 2, 3):
        from_y[d] = [
            make(
                kv.at[d, 0, :, mine, :], kv.at[d, 0, :, mine, :],
                fsem.at[d - 1, f], frsem.at[d - 1, f], dev(dy=f), has[d],
            )
            for f in (2, 1, 3)
        ]
    for f in (2, 1, 3, 0):
        from_y[2].append(
            make(
                kv.at[2, 0, :, mine, :], kv.at[2, 1, :, mine, :],
                psem.at[f], prsem.at[f], dev(dcore=1, dy=f), has[2],
            )
        )

    from_core.wait_recv()
    for c in from_x:
        c.wait_recv()
    part[...] = forward(0)
    for d in (1, 3, 2):

        @pl.when(has[d])
        def _():
            from_z[d][0].wait_recv()
            for c in from_y[d]:
                c.start()

    def hand_on(d, arriving):
        @pl.when(has[d])
        def _():
            for c in arriving:
                c.wait_recv()
            passed[d].start()

    def use(d):
        @pl.when(has[d])
        def _():
            passed[d].wait_recv()
            part[...] += forward(d)

    hand_on(1, from_y[1])
    hand_on(3, from_y[3])
    use(1)
    use(3)

    @pl.when(has[2])
    def _():
        for c in from_y[2]:
            c.wait_recv()
        part[...] += forward(2)


    arrivals = []
    for e in (2, 1, 3):
        parts[e - 1] = part[pl.ds(e * ROWS, ROWS), :].astype(BF)
        arrivals.append(
            started(make(parts.at[e - 1], partr.at[e - 1], nsem.at[e - 1], nrsem.at[e - 1], dev(dx=e)))
        )
    for c in arrivals:
        c.wait_recv()
    numerator = part[pl.ds(0, ROWS), :]
    for e in range(3):
        numerator = numerator + partr[e].astype(F32)
    root_mean = jnp.sqrt(jnp.mean(numerator * numerator, axis=-1, keepdims=True) + EPSILON)
    normed = numerator / root_mean
    grad = gbuf[...].astype(F32)
    ngall[0] = ((grad - normed * jnp.mean(grad * normed, axis=-1, keepdims=True)) / root_mean).astype(BF)
    from_x = [
        started(make(ngall.at[0], ngall.at[4 - e], gsem.at[e - 1], grsem.at[e - 1], dev(dx=e)))
        for e in (2, 1, 3)
    ]
    out_ref[0] = normed.astype(BF)
    for c in from_x:
        c.wait_recv()

    passed, from_y = {}, {}
    for d in range(4):
        from_y[d] = []
        if d == 2:
            for r in (0, 1):
                for f in (2, 1, 3, 0):
                    if (r, f) != (0, 0):
                        rows = pl.ds(pl.multiple_of(((y + f) % 4) * 32, 32), 32)
                        from_y[d].append(
                            make(
                                dkvs.at[d, r, :, rows, :], yr.at[d + 2 * r, f],
                                ysem.at[d + 2 * r, f], yrsem.at[d + 2 * r, f], dev(dcore=r, dy=f), has[d],
                            )
                        )
            continue
        passed[d] = make(dkvs.at[d, 1], cr.at[d], ysem.at[d, 0], yrsem.at[d, 0], dev(dcore=1), has[d])
        for f in (2, 1, 3):
            rows = pl.ds(pl.multiple_of(((y + f) % 4) * 32, 32), 32)
            from_y[d].append(
                make(ys.at[d, :, rows, :], yr.at[d, f], ysem.at[d, f], yrsem.at[d, f], dev(dy=f), has[d])
            )

    def backward(d):
        @pl.when(has[d])
        def _():
            queries = qall[...].reshape(4 * ROWS, D)
            grads = ngall[...].reshape(4 * ROWS, D)
            keys = kv[d, :, 0].reshape(2 * ROWS, D)
            values = kv[d, :, 1].reshape(2 * ROWS, D)
            coefficient = (2.0 * s_ref[d] * dot_last(grads, values)).astype(BF)
            dkvs[d, :, 0] = dot_first(coefficient, queries).astype(BF).reshape(2, ROWS, D)
            dkvs[d, :, 1] = dot_first(w_ref[d], grads).astype(BF).reshape(2, ROWS, D)
            for c in from_y[2] if d == 2 else (passed[d],):
                c.start()
            dqacc[...] += dot(coefficient, keys)

    def over_y(d):
        @pl.when(has[d])
        def _():
            passed[d].wait_recv()
            ys[d] = (dkvs[d, 0].astype(F32) + cr[d].astype(F32)).astype(BF)
            for c in from_y[d]:
                c.start()

    dqacc[...] = jnp.zeros_like(dqacc)
    late = []
    for d in BACK:
        backward(d)
        if d != 2:
            late.append(d)
        if len(late) > 2:
            over_y(late.pop(0))
    for d in late:
        over_y(d)
    arrivals = []
    for e in (2, 1, 3):
        dqs[e - 1] = dqacc[pl.ds(e * ROWS, ROWS), :].astype(BF)
        arrivals.append(
            started(make(dqs.at[e - 1], dqr.at[e - 1], dsem.at[e - 1], drsem.at[e - 1], dev(dx=e)))
        )

    to_z = {}
    other = {o: zlo != o for o in (0, 1)}
    for d in BACK:
        to_z[d] = []
        for o in (0, 1):
            only = has[d] if d else other[o]
            c = make(
                zs.at[d, o], zr.at[d * 4 + zlo], asem.at[d * 2 + o], arsem.at[d * 4 + zlo],
                dev(dzhi=4 - d, dzlo=o + 4 - zlo), only,
            )
            to_z[d].append((c, only))

        @pl.when(has[d])
        def _():
            for c in from_y[d]:
                c.wait_recv()
            total = (dkvs[d, 0, :, mine, :] if d == 2 else ys[d, :, mine, :]).astype(F32)
            for i in range(1, 4):
                total = total + yr[d, i].astype(F32)
            if d == 2:
                for i in range(4):
                    total = total + yr[4, i].astype(F32)
            zs[d] = total.astype(BF)
            for c, only in to_z[d]:
                if d:
                    c.start()
                else:
                    pl.when(only)(c.start)

    for c in arrivals:
        c.wait_recv()
    query_grad = dqacc[pl.ds(0, ROWS), :]
    for e in range(3):
        query_grad = query_grad + dqr[e].astype(F32)
    out_ref[1] = query_grad.astype(BF)

    def arrived(c):
        pltpu.make_async_remote_copy(
            src_ref=zs.at[0, 0], dst_ref=c[0], send_sem=asem.at[0], recv_sem=c[1],
            device_id=dev(dcore=1), device_id_type=MESH,
        ).wait_recv()

    place = pl.ds(pl.multiple_of(y * 32, 32), 32)
    last = []
    for k in range(4):
        for f in (2, 1, 3, 0):
            only = owner if f else jnp.logical_and(owner, zlo != k)
            c = make(
                fin, out_ref.at[2 + zlo % 2, place, :], osem.at[k * 4 + f], orsem.at[f * 2 + zlo % 2],
                dev(dy=f, dzlo=k + 4 - zlo), only,
            )
            last.append((c, only))

    @pl.when(owner)
    def _():
        zr[zlo] = zs[0, zlo % 2]
        for k in range(4):

            @pl.when(zlo != k)
            def _():
                arrived((zr.at[k], arsem.at[k]))

        for d in (1, 3, 2):

            @pl.when(feeds[d])
            def _():
                for k in range(4):
                    arrived((zr.at[d * 4 + k], arsem.at[d * 4 + k]))

        total = zr[0].astype(F32)
        for i in range(1, 16):
            total = total + zr[i].astype(F32)
        fin[...] = total.astype(BF)
        for c, only in last:
            if only is owner:
                c.start()
            else:
                pl.when(only)(c.start)
        out_ref[2 + zlo % 2, place, :] = total.astype(BF)

    for o in (0, 1):
        for f in range(4):
            rows = pl.ds(pl.multiple_of(((y + 4 - f) % 4) * 32, 32), 32)
            wait = functools.partial(arrived, (out_ref.at[2 + o, rows, :], orsem.at[f * 2 + o]))
            if f:
                wait()
            else:
                pl.when(zlo != o)(wait)
    groups = []
    for c, only in sent:
        if only is None:
            c.wait_send()
        elif any(o is only for o, _ in groups):
            next(g for o, g in groups if o is only).append(c)
        else:
            groups.append((only, [c]))
    for only, group in groups:

        @pl.when(only)
        def _():
            for c in group:
                c.wait_send()


def local(query_rows, key_rows, value_rows, out_grad):
    dma = pltpu.SemaphoreType.DMA
    packed = pl.pallas_call(
        kernel,
        out_shape=jax.ShapeDtypeStruct((4, ROWS, D), BF),
        in_specs=[pl.BlockSpec(memory_space=pltpu.VMEM)],
        out_specs=pl.BlockSpec(memory_space=pltpu.VMEM),
        scratch_shapes=[
            pltpu.VMEM((4, ROWS, D), BF),
            pltpu.VMEM((4, ROWS, D), BF),
            pltpu.VMEM((ROWS, D), BF),
            pltpu.VMEM((4, 2, 2, ROWS, D), BF),
            pltpu.VMEM((4, 4 * ROWS, 2 * ROWS), F32),
            pltpu.VMEM((4, 4 * ROWS, 2 * ROWS), BF),
            pltpu.VMEM((4 * ROWS, D), F32),
            pltpu.VMEM((3, ROWS, D), BF),
            pltpu.VMEM((3, ROWS, D), BF),
            pltpu.VMEM((4 * ROWS, D), F32),
            pltpu.VMEM((3, ROWS, D), BF),
            pltpu.VMEM((3, ROWS, D), BF),
            pltpu.VMEM((4, 2, 2, ROWS, D), BF),
            pltpu.VMEM((4, 2, ROWS, D), BF),
            pltpu.VMEM((4, 2, ROWS, D), BF),
            pltpu.VMEM((5, 4, 2, 32, D), BF),
            pltpu.VMEM((4, 2, 32, D), BF),
            pltpu.VMEM((16, 32, D), BF),
            pltpu.VMEM((32, D), BF),
            dma((4,)), dma((3,)), dma((3,)), dma((6,)), dma((3,)), dma((3,)), dma((3, 4)), dma((3, 4)), dma((4,)), dma((4,)),
            dma((3,)), dma((3,)), dma((3,)), dma((3,)), dma((3,)), dma((3,)),
            dma((5, 4)), dma((5, 4)), dma((8,)), dma((16,)), dma((16,)), dma((8,)),
        ],
        compiler_params=pltpu.CompilerParams(
            collective_id=0, has_side_effects=True, vmem_limit_bytes=48 * 2**20
        ),
    )(jnp.stack((query_rows, key_rows, value_rows, out_grad)))
    return packed[0], packed[1], packed[2], packed[3]


def solution(mesh):
    return jax.shard_map(
        local,
        mesh=mesh,
        in_specs=(P("seq", "head"), P("seq", None), P("seq", None), P("seq", "head")),
        out_specs=(P("seq", "head"), P("seq", "head"), P("seq", None), P("seq", None)),
        check_vma=False,
    )
```

```python
import functools

import jax
import jax.numpy as jnp
from jax import lax
from jax.experimental import pallas as pl
from jax.experimental.pallas import tpu as pltpu
from jax.sharding import PartitionSpec as P

MESH = pl.DeviceIdType.MESH
EPSILON = 1e-06
BF = jnp.bfloat16
F32 = jnp.float32
ROWS = 128
D = 128
BACK = (2, 3, 1, 0)


def dot_last(a, b):
    return lax.dot_general(a, b, (((1,), (1,)), ((), ())), preferred_element_type=F32)


def dot_first(a, b):
    return lax.dot_general(a, b, (((0,), (0,)), ((), ())), preferred_element_type=F32)


def dot(a, b):
    return jnp.dot(a, b, preferred_element_type=F32)


def kernel(
    in_ref,
    out_ref,
    qall, ngall, gbuf, kv, s_ref, w_ref, part, parts, partr,
    dqacc, dqs, dqr, dkvs, cr, ys, yr, zs, zr, fin,
    lsem, zsem, zrsem, csem, qsem, qrsem, fsem, frsem, psem, prsem,
    nsem, nrsem, gsem, grsem, dsem, drsem, ysem, yrsem, asem, arsem, osem, orsem,
):
    seq, head = lax.axis_index("seq"), lax.axis_index("head")
    zhi, x, core = seq // 8, (seq // 2) % 4, seq % 2
    zlo, y = head // 4, head % 4

    def dev(dzhi=0, dx=0, dcore=0, dzlo=0, dy=0):
        return (
            (((zhi + dzhi) % 4) * 4 + (x + dx) % 4) * 2 + (core + dcore) % 2,
            ((zlo + dzlo) % 4) * 4 + (y + dy) % 4,
        )

    has = {d: zhi >= d for d in range(4)}
    feeds = {d: zhi + d <= 3 for d in range(4)}

    near = [dev(dzlo=m) for m in (1, 2, 3)]
    near += [dev(dy=f, dzlo=m) for f in (1, 2, 3) for m in (1, 2, 3)]
    near += [dev(dx=e) for e in (1, 2, 3)]
    near += [dev(dcore=r, dy=f) for r in (0, 1) for f in range(4) if (r, f) != (0, 0)]
    zr[...] = jnp.zeros_like(zr)
    barrier = pltpu.get_barrier_semaphore()
    owner = zlo < 2
    for d in (2, 3, 1):

        @pl.when(has[d])
        def _():
            pl.semaphore_signal(barrier, 1, device_id=dev(dzhi=4 - d), device_id_type=MESH)

    for d in (1, 2, 3):

        @pl.when(jnp.logical_and(feeds[d], owner))
        def _():
            for m in range(4):
                pl.semaphore_signal(barrier, 1, device_id=dev(dzhi=d, dzlo=m), device_id_type=MESH)

    for p in near:
        pl.semaphore_signal(barrier, 1, device_id=p, device_id_type=MESH)
    loads = [
        pltpu.make_async_copy(in_ref.at[1], kv.at[0, 0, 0], lsem.at[0]),
        pltpu.make_async_copy(in_ref.at[2], kv.at[0, 0, 1], lsem.at[1]),
        pltpu.make_async_copy(in_ref.at[0], qall.at[0], lsem.at[2]),
        pltpu.make_async_copy(in_ref.at[3], gbuf, lsem.at[3]),
    ]
    for c in loads:
        c.start()
    for c in loads:
        c.wait()
    pl.semaphore_wait(barrier, len(near) + (3 - zhi) + 2 * zhi)

    sent = []

    def make(src, dst, ssem, rsem, to, only=None):
        c = pltpu.make_async_remote_copy(
            src_ref=src, dst_ref=dst, send_sem=ssem, recv_sem=rsem, device_id=to, device_id_type=MESH
        )
        sent.append((c, only))
        return c

    def started(c):
        c.start()
        return c

    mine = pl.ds(pl.multiple_of(y * 32, 32), 32)
    from_z = {}
    for d in (1, 2, 3):
        from_z[d] = [
            make(
                kv.at[0, 0, :, mine, :], kv.at[d, 0, :, mine, :],
                zsem.at[d - 1], zrsem.at[d - 1], dev(dzhi=d), feeds[d],
            )
        ]
    for d in (2, 3, 1):

        @pl.when(feeds[d])
        def _():
            for c in from_z[d]:
                c.start()

    from_core = started(make(kv.at[0, 0], kv.at[0, 1], csem.at[0], csem.at[1], dev(dcore=1)))
    from_x = [
        started(make(qall.at[0], qall.at[4 - e], qsem.at[e - 1], qrsem.at[e - 1], dev(dx=e)))
        for e in (2, 1, 3)
    ]

    gap = lax.broadcasted_iota(jnp.int32, (ROWS, ROWS), 1) - lax.broadcasted_iota(
        jnp.int32, (ROWS, ROWS), 0
    )

    def limit(e, r):
        return (((x + e) % 4 - x) * 2 + core - (core + r) % 2) * ROWS

    def forward(d, first=0, count=4):
        queries = qall[first : first + count].reshape(count * ROWS, D)
        keys = kv[d, :, 0].reshape(2 * ROWS, D)
        values = kv[d, :, 1].reshape(2 * ROWS, D)
        products = dot_last(queries, keys)
        if d == 0:
            products = jnp.concatenate(
                [
                    jnp.concatenate(
                        [
                            jnp.where(
                                gap <= limit(e, r),
                                products[e * ROWS : (e + 1) * ROWS, r * ROWS : (r + 1) * ROWS],
                                0.0,
                            )
                            for r in range(2)
                        ],
                        axis=1,
                    )
                    for e in range(4)
                ],
                axis=0,
            )
        return dot((products * products).astype(BF), values)

    def keep(d):
        queries = qall[...].reshape(4 * ROWS, D)
        keys = kv[d, :, 0].reshape(2 * ROWS, D)
        products = dot_last(keys, queries)
        for e in range(4):
            for r in range(2):
                tile = products[r * ROWS : (r + 1) * ROWS, e * ROWS : (e + 1) * ROWS]
                if d == 0:
                    tile = jnp.where(-gap <= limit(e, r), tile, 0.0)
                s_ref[d, pl.ds(r * ROWS, ROWS), pl.ds(e * ROWS, ROWS)] = 2.0 * tile
                w_ref[d, pl.ds(r * ROWS, ROWS), pl.ds(e * ROWS, ROWS)] = (tile * tile).astype(BF)

    passed, from_y = {}, {}
    for d in (1, 3):
        passed[d] = make(
            kv.at[d, 0], kv.at[d, 1], csem.at[d + 1], csem.at[d + 2], dev(dcore=1), has[d]
        )
    for d in (1, 2, 3):
        from_y[d] = [
            make(
                kv.at[d, 0, :, mine, :], kv.at[d, 0, :, mine, :],
                fsem.at[d - 1, f], frsem.at[d - 1, f], dev(dy=f), has[d],
            )
            for f in (2, 1, 3)
        ]
    for f in (2, 1, 3, 0):
        from_y[2].append(
            make(
                kv.at[2, 0, :, mine, :], kv.at[2, 1, :, mine, :],
                psem.at[f], prsem.at[f], dev(dcore=1, dy=f), has[2],
            )
        )

    from_core.wait_recv()
    for c in from_x:
        c.wait_recv()
    part[...] = forward(0)
    for d in (1, 3, 2):

        @pl.when(has[d])
        def _():
            from_z[d][0].wait_recv()
            for c in from_y[d]:
                c.start()

    def hand_on(d, arriving):
        @pl.when(has[d])
        def _():
            for c in arriving:
                c.wait_recv()
            passed[d].start()

    def use(d):
        @pl.when(has[d])
        def _():
            passed[d].wait_recv()
            part[...] += forward(d)

    hand_on(1, from_y[1])
    hand_on(3, from_y[3])
    use(1)
    use(3)

    @pl.when(has[2])
    def _():
        for c in from_y[2]:
            c.wait_recv()


    arrivals = []

    @pl.when(has[2])
    def _():
        part[...] += forward(2)

    for e in (2, 1, 3):
        if e:
            parts[e - 1] = part[pl.ds(e * ROWS, ROWS), :].astype(BF)
            arrivals.append(
                started(
                    make(parts.at[e - 1], partr.at[e - 1], nsem.at[e - 1], nrsem.at[e - 1], dev(dx=e))
                )
            )
    pl.when(has[2])(functools.partial(keep, 2))
    pl.when(has[3])(functools.partial(keep, 3))
    for c in arrivals:
        c.wait_recv()
    numerator = part[pl.ds(0, ROWS), :]
    for e in range(3):
        numerator = numerator + partr[e].astype(F32)
    root_mean = jnp.sqrt(jnp.mean(numerator * numerator, axis=-1, keepdims=True) + EPSILON)
    normed = numerator / root_mean
    grad = gbuf[...].astype(F32)
    ngall[0] = ((grad - normed * jnp.mean(grad * normed, axis=-1, keepdims=True)) / root_mean).astype(BF)
    from_x = [
        started(make(ngall.at[0], ngall.at[4 - e], gsem.at[e - 1], grsem.at[e - 1], dev(dx=e)))
        for e in (2, 1, 3)
    ]
    out_ref[0] = normed.astype(BF)
    pl.when(has[1])(functools.partial(keep, 1))
    keep(0)
    for c in from_x:
        c.wait_recv()

    passed, from_y = {}, {}
    for d in range(4):
        from_y[d] = []
        if d == 2:
            for r in (0, 1):
                for f in (2, 1, 3, 0):
                    if (r, f) != (0, 0):
                        rows = pl.ds(pl.multiple_of(((y + f) % 4) * 32, 32), 32)
                        from_y[d].append(
                            make(
                                dkvs.at[d, r, :, rows, :], yr.at[d + 2 * r, f],
                                ysem.at[d + 2 * r, f], yrsem.at[d + 2 * r, f], dev(dcore=r, dy=f), has[d],
                            )
                        )
            continue
        passed[d] = make(dkvs.at[d, 1], cr.at[d], ysem.at[d, 0], yrsem.at[d, 0], dev(dcore=1), has[d])
        for f in (2, 1, 3):
            rows = pl.ds(pl.multiple_of(((y + f) % 4) * 32, 32), 32)
            from_y[d].append(
                make(ys.at[d, :, rows, :], yr.at[d, f], ysem.at[d, f], yrsem.at[d, f], dev(dy=f), has[d])
            )

    def backward(d):
        @pl.when(has[d])
        def _():
            queries = qall[...].reshape(4 * ROWS, D)
            grads = ngall[...].reshape(4 * ROWS, D)
            keys = kv[d, :, 0].reshape(2 * ROWS, D)
            values = kv[d, :, 1].reshape(2 * ROWS, D)
            coefficient = (s_ref[d] * dot_last(values, grads)).astype(BF)
            dkvs[d, :, 0] = dot(coefficient, queries).astype(BF).reshape(2, ROWS, D)
            dkvs[d, :, 1] = dot(w_ref[d], grads).astype(BF).reshape(2, ROWS, D)
            for c in from_y[2] if d == 2 else (passed[d],):
                c.start()
            dqacc[...] += dot_first(coefficient, keys)

    def over_y(d):
        @pl.when(has[d])
        def _():
            passed[d].wait_recv()
            ys[d] = (dkvs[d, 0].astype(F32) + cr[d].astype(F32)).astype(BF)
            for c in from_y[d]:
                c.start()

    dqacc[...] = jnp.zeros_like(dqacc)
    late = []
    for d in BACK:
        backward(d)
        if d != 2:
            late.append(d)
        if len(late) > 2:
            over_y(late.pop(0))
    for d in late:
        over_y(d)
    arrivals = []
    for e in (2, 1, 3):
        dqs[e - 1] = dqacc[pl.ds(e * ROWS, ROWS), :].astype(BF)
        arrivals.append(
            started(make(dqs.at[e - 1], dqr.at[e - 1], dsem.at[e - 1], drsem.at[e - 1], dev(dx=e)))
        )

    to_z = {}
    other = {o: zlo != o for o in (0, 1)}
    for d in BACK:
        to_z[d] = []
        for o in (0, 1):
            only = has[d] if d else other[o]
            c = make(
                zs.at[d, o], zr.at[d * 4 + zlo], asem.at[d * 2 + o], arsem.at[d * 4 + zlo],
                dev(dzhi=4 - d, dzlo=o + 4 - zlo), only,
            )
            to_z[d].append((c, only))

        @pl.when(has[d])
        def _():
            for c in from_y[d]:
                c.wait_recv()
            total = (dkvs[d, 0, :, mine, :] if d == 2 else ys[d, :, mine, :]).astype(F32)
            for i in range(1, 4):
                total = total + yr[d, i].astype(F32)
            if d == 2:
                for i in range(4):
                    total = total + yr[4, i].astype(F32)
            zs[d] = total.astype(BF)
            for c, only in to_z[d]:
                if d:
                    c.start()
                else:
                    pl.when(only)(c.start)

    for c in arrivals:
        c.wait_recv()
    query_grad = dqacc[pl.ds(0, ROWS), :]
    for e in range(3):
        query_grad = query_grad + dqr[e].astype(F32)
    out_ref[1] = query_grad.astype(BF)

    def arrived(c):
        pltpu.make_async_remote_copy(
            src_ref=zs.at[0, 0], dst_ref=c[0], send_sem=asem.at[0], recv_sem=c[1],
            device_id=dev(dcore=1), device_id_type=MESH,
        ).wait_recv()

    place = pl.ds(pl.multiple_of(y * 32, 32), 32)
    last = []
    for k in range(4):
        for f in (2, 1, 3, 0):
            only = owner if f else jnp.logical_and(owner, zlo != k)
            c = make(
                fin, out_ref.at[2 + zlo % 2, place, :], osem.at[k * 4 + f], orsem.at[f * 2 + zlo % 2],
                dev(dy=f, dzlo=k + 4 - zlo), only,
            )
            last.append((c, only))

    @pl.when(owner)
    def _():
        zr[zlo] = zs[0, zlo % 2]
        for k in range(4):

            @pl.when(zlo != k)
            def _():
                arrived((zr.at[k], arsem.at[k]))

        for d in (1, 3, 2):

            @pl.when(feeds[d])
            def _():
                for k in range(4):
                    arrived((zr.at[d * 4 + k], arsem.at[d * 4 + k]))

        total = zr[0].astype(F32)
        for i in range(1, 16):
            total = total + zr[i].astype(F32)
        fin[...] = total.astype(BF)
        for c, only in last:
            if only is owner:
                c.start()
            else:
                pl.when(only)(c.start)
        out_ref[2 + zlo % 2, place, :] = total.astype(BF)

    for o in (0, 1):
        for f in range(4):
            rows = pl.ds(pl.multiple_of(((y + 4 - f) % 4) * 32, 32), 32)
            wait = functools.partial(arrived, (out_ref.at[2 + o, rows, :], orsem.at[f * 2 + o]))
            if f:
                wait()
            else:
                pl.when(zlo != o)(wait)
    groups = []
    for c, only in sent:
        if only is None:
            c.wait_send()
        elif any(o is only for o, _ in groups):
            next(g for o, g in groups if o is only).append(c)
        else:
            groups.append((only, [c]))
    for only, group in groups:

        @pl.when(only)
        def _():
            for c in group:
                c.wait_send()


def local(query_rows, key_rows, value_rows, out_grad):
    dma = pltpu.SemaphoreType.DMA
    packed = pl.pallas_call(
        kernel,
        out_shape=jax.ShapeDtypeStruct((4, ROWS, D), BF),
        in_specs=[pl.BlockSpec(memory_space=pltpu.VMEM)],
        out_specs=pl.BlockSpec(memory_space=pltpu.VMEM),
        scratch_shapes=[
            pltpu.VMEM((4, ROWS, D), BF),
            pltpu.VMEM((4, ROWS, D), BF),
            pltpu.VMEM((ROWS, D), BF),
            pltpu.VMEM((4, 2, 2, ROWS, D), BF),
            pltpu.VMEM((4, 2 * ROWS, 4 * ROWS), F32),
            pltpu.VMEM((4, 2 * ROWS, 4 * ROWS), BF),
            pltpu.VMEM((4 * ROWS, D), F32),
            pltpu.VMEM((3, ROWS, D), BF),
            pltpu.VMEM((3, ROWS, D), BF),
            pltpu.VMEM((4 * ROWS, D), F32),
            pltpu.VMEM((3, ROWS, D), BF),
            pltpu.VMEM((3, ROWS, D), BF),
            pltpu.VMEM((4, 2, 2, ROWS, D), BF),
            pltpu.VMEM((4, 2, ROWS, D), BF),
            pltpu.VMEM((4, 2, ROWS, D), BF),
            pltpu.VMEM((5, 4, 2, 32, D), BF),
            pltpu.VMEM((4, 2, 32, D), BF),
            pltpu.VMEM((16, 32, D), BF),
            pltpu.VMEM((32, D), BF),
            dma((4,)), dma((3,)), dma((3,)), dma((6,)), dma((3,)), dma((3,)), dma((3, 4)), dma((3, 4)), dma((4,)), dma((4,)),
            dma((3,)), dma((3,)), dma((3,)), dma((3,)), dma((3,)), dma((3,)),
            dma((5, 4)), dma((5, 4)), dma((8,)), dma((16,)), dma((16,)), dma((8,)),
        ],
        compiler_params=pltpu.CompilerParams(
            collective_id=0, has_side_effects=True, vmem_limit_bytes=48 * 2**20
        ),
    )(jnp.stack((query_rows, key_rows, value_rows, out_grad)))
    return packed[0], packed[1], packed[2], packed[3]


def solution(mesh):
    return jax.shard_map(
        local,
        mesh=mesh,
        in_specs=(P("seq", "head"), P("seq", None), P("seq", None), P("seq", "head")),
        out_specs=(P("seq", "head"), P("seq", "head"), P("seq", None), P("seq", None)),
        check_vma=False,
    )
```

```python
import functools

import jax
import jax.numpy as jnp
from jax import lax
from jax.experimental import pallas as pl
from jax.experimental.pallas import tpu as pltpu
from jax.sharding import PartitionSpec as P

MESH = pl.DeviceIdType.MESH
EPSILON = 1e-06
BF = jnp.bfloat16
F32 = jnp.float32
ROWS = 128
D = 128
BACK = (2, 3, 1, 0)


def dot_last(a, b):
    return lax.dot_general(a, b, (((1,), (1,)), ((), ())), preferred_element_type=F32)


def dot_first(a, b):
    return lax.dot_general(a, b, (((0,), (0,)), ((), ())), preferred_element_type=F32)


def dot(a, b):
    return jnp.dot(a, b, preferred_element_type=F32)


def kernel(
    in_ref,
    out_ref,
    qall, ngall, gbuf, kv, s_ref, w_ref, part, parts, partr,
    dqacc, dqs, dqr, dkvs, cr, ys, yr, zs, zr, fin,
    lsem, zsem, zrsem, csem, qsem, qrsem, fsem, frsem, psem, prsem,
    nsem, nrsem, gsem, grsem, dsem, drsem, ysem, yrsem, asem, arsem, osem, orsem,
):
    seq, head = lax.axis_index("seq"), lax.axis_index("head")
    zhi, x, core = seq // 8, (seq // 2) % 4, seq % 2
    zlo, y = head // 4, head % 4

    def dev(dzhi=0, dx=0, dcore=0, dzlo=0, dy=0):
        return (
            (((zhi + dzhi) % 4) * 4 + (x + dx) % 4) * 2 + (core + dcore) % 2,
            ((zlo + dzlo) % 4) * 4 + (y + dy) % 4,
        )

    has = {d: zhi >= d for d in range(4)}
    feeds = {d: zhi + d <= 3 for d in range(4)}

    near = [dev(dzlo=m) for m in (1, 2, 3)]
    near += [dev(dy=f, dzlo=m) for f in (1, 2, 3) for m in (1, 2, 3)]
    near += [dev(dx=e) for e in (1, 2, 3)]
    near += [dev(dcore=r, dy=f) for r in (0, 1) for f in range(4) if (r, f) != (0, 0)]
    zr[...] = jnp.zeros_like(zr)
    barrier = pltpu.get_barrier_semaphore()
    owner = zlo < 2
    for d in (2, 3, 1):

        @pl.when(has[d])
        def _():
            pl.semaphore_signal(barrier, 1, device_id=dev(dzhi=4 - d), device_id_type=MESH)

    for d in (1, 2, 3):

        @pl.when(jnp.logical_and(feeds[d], owner))
        def _():
            for m in range(4):
                pl.semaphore_signal(barrier, 1, device_id=dev(dzhi=d, dzlo=m), device_id_type=MESH)

    for p in near:
        pl.semaphore_signal(barrier, 1, device_id=p, device_id_type=MESH)
    loads = [
        pltpu.make_async_copy(in_ref.at[1], kv.at[0, 0, 0], lsem.at[0]),
        pltpu.make_async_copy(in_ref.at[2], kv.at[0, 0, 1], lsem.at[1]),
        pltpu.make_async_copy(in_ref.at[0], qall.at[0], lsem.at[2]),
        pltpu.make_async_copy(in_ref.at[3], gbuf, lsem.at[3]),
    ]
    for c in loads:
        c.start()
    for c in loads:
        c.wait()
    pl.semaphore_wait(barrier, len(near) + (3 - zhi) + 2 * zhi)

    sent = []

    def make(src, dst, ssem, rsem, to, only=None):
        c = pltpu.make_async_remote_copy(
            src_ref=src, dst_ref=dst, send_sem=ssem, recv_sem=rsem, device_id=to, device_id_type=MESH
        )
        sent.append((c, only))
        return c

    def started(c):
        c.start()
        return c

    mine = pl.ds(pl.multiple_of(y * 32, 32), 32)
    from_z = {}
    for d in (1, 2, 3):
        from_z[d] = [
            make(
                kv.at[0, 0, :, mine, :], kv.at[d, 0, :, mine, :],
                zsem.at[d - 1], zrsem.at[d - 1], dev(dzhi=d), feeds[d],
            )
        ]
    for d in (2, 3, 1):

        @pl.when(feeds[d])
        def _():
            for c in from_z[d]:
                c.start()

    from_core = started(make(kv.at[0, 0], kv.at[0, 1], csem.at[0], csem.at[1], dev(dcore=1)))
    from_x = [
        started(make(qall.at[0], qall.at[4 - e], qsem.at[e - 1], qrsem.at[e - 1], dev(dx=e)))
        for e in (2, 1, 3)
    ]

    gap = lax.broadcasted_iota(jnp.int32, (ROWS, ROWS), 1) - lax.broadcasted_iota(
        jnp.int32, (ROWS, ROWS), 0
    )

    def limit(e, r):
        return (((x + e) % 4 - x) * 2 + core - (core + r) % 2) * ROWS

    def forward(d, first=0, count=4):
        queries = qall[first : first + count].reshape(count * ROWS, D)
        keys = kv[d, :, 0].reshape(2 * ROWS, D)
        values = kv[d, :, 1].reshape(2 * ROWS, D)
        products = dot_last(queries, keys)
        if d == 0:
            products = jnp.concatenate(
                [
                    jnp.concatenate(
                        [
                            jnp.where(
                                gap <= limit(e, r),
                                products[e * ROWS : (e + 1) * ROWS, r * ROWS : (r + 1) * ROWS],
                                0.0,
                            )
                            for r in range(2)
                        ],
                        axis=1,
                    )
                    for e in range(4)
                ],
                axis=0,
            )
        return dot((products * products).astype(BF), values)

    def keep(d):
        queries = qall[...].reshape(4 * ROWS, D)
        keys = kv[d, :, 0].reshape(2 * ROWS, D)
        products = dot_last(keys, queries)
        for e in range(4):
            for r in range(2):
                tile = products[r * ROWS : (r + 1) * ROWS, e * ROWS : (e + 1) * ROWS]
                tile = jnp.where(-gap <= limit(e, r) + d * (8 * ROWS), tile, 0.0)
                s_ref[d, pl.ds(r * ROWS, ROWS), pl.ds(e * ROWS, ROWS)] = 2.0 * tile
                w_ref[d, pl.ds(r * ROWS, ROWS), pl.ds(e * ROWS, ROWS)] = (tile * tile).astype(BF)

    passed, from_y = {}, {}
    for d in (1, 3):
        passed[d] = make(
            kv.at[d, 0], kv.at[d, 1], csem.at[d + 1], csem.at[d + 2], dev(dcore=1), has[d]
        )
    for d in (1, 2, 3):
        from_y[d] = [
            make(
                kv.at[d, 0, :, mine, :], kv.at[d, 0, :, mine, :],
                fsem.at[d - 1, f], frsem.at[d - 1, f], dev(dy=f), has[d],
            )
            for f in (2, 1, 3)
        ]
    for f in (2, 1, 3, 0):
        from_y[2].append(
            make(
                kv.at[2, 0, :, mine, :], kv.at[2, 1, :, mine, :],
                psem.at[f], prsem.at[f], dev(dcore=1, dy=f), has[2],
            )
        )

    from_core.wait_recv()
    for c in from_x:
        c.wait_recv()
    part[...] = forward(0)
    for d in (1, 3, 2):

        @pl.when(has[d])
        def _():
            from_z[d][0].wait_recv()
            for c in from_y[d]:
                c.start()

    def hand_on(d, arriving):
        @pl.when(has[d])
        def _():
            for c in arriving:
                c.wait_recv()
            passed[d].start()

    def use(d):
        @pl.when(has[d])
        def _():
            passed[d].wait_recv()
            part[...] += forward(d)

    hand_on(1, from_y[1])
    hand_on(3, from_y[3])
    use(1)
    use(3)

    @pl.when(has[2])
    def _():
        for c in from_y[2]:
            c.wait_recv()


    arrivals = []

    @pl.when(has[2])
    def _():
        part[...] += forward(2)

    for e in (2, 1, 3):
        if e:
            parts[e - 1] = part[pl.ds(e * ROWS, ROWS), :].astype(BF)
            arrivals.append(
                started(
                    make(parts.at[e - 1], partr.at[e - 1], nsem.at[e - 1], nrsem.at[e - 1], dev(dx=e))
                )
            )
    lax.fori_loop(1, zhi + 1, lambda d, _: (keep(d), 0)[1], 0)
    for c in arrivals:
        c.wait_recv()
    numerator = part[pl.ds(0, ROWS), :]
    for e in range(3):
        numerator = numerator + partr[e].astype(F32)
    root_mean = jnp.sqrt(jnp.mean(numerator * numerator, axis=-1, keepdims=True) + EPSILON)
    normed = numerator / root_mean
    grad = gbuf[...].astype(F32)
    ngall[0] = ((grad - normed * jnp.mean(grad * normed, axis=-1, keepdims=True)) / root_mean).astype(BF)
    from_x = [
        started(make(ngall.at[0], ngall.at[4 - e], gsem.at[e - 1], grsem.at[e - 1], dev(dx=e)))
        for e in (2, 1, 3)
    ]
    out_ref[0] = normed.astype(BF)
    keep(0)
    for c in from_x:
        c.wait_recv()

    passed, from_y = {}, {}
    for d in range(4):
        from_y[d] = []
        if d == 2:
            for r in (0, 1):
                for f in (2, 1, 3, 0):
                    if (r, f) != (0, 0):
                        rows = pl.ds(pl.multiple_of(((y + f) % 4) * 32, 32), 32)
                        from_y[d].append(
                            make(
                                dkvs.at[d, r, :, rows, :], yr.at[d + 2 * r, f],
                                ysem.at[d + 2 * r, f], yrsem.at[d + 2 * r, f], dev(dcore=r, dy=f), has[d],
                            )
                        )
            continue
        passed[d] = make(dkvs.at[d, 1], cr.at[d], ysem.at[d, 0], yrsem.at[d, 0], dev(dcore=1), has[d])
        for f in (2, 1, 3):
            rows = pl.ds(pl.multiple_of(((y + f) % 4) * 32, 32), 32)
            from_y[d].append(
                make(ys.at[d, :, rows, :], yr.at[d, f], ysem.at[d, f], yrsem.at[d, f], dev(dy=f), has[d])
            )

    def backward(d):
        @pl.when(has[d])
        def _():
            queries = qall[...].reshape(4 * ROWS, D)
            grads = ngall[...].reshape(4 * ROWS, D)
            keys = kv[d, :, 0].reshape(2 * ROWS, D)
            values = kv[d, :, 1].reshape(2 * ROWS, D)
            coefficient = (s_ref[d] * dot_last(values, grads)).astype(BF)
            dkvs[d, :, 0] = dot(coefficient, queries).astype(BF).reshape(2, ROWS, D)
            dkvs[d, :, 1] = dot(w_ref[d], grads).astype(BF).reshape(2, ROWS, D)
            for c in from_y[2] if d == 2 else (passed[d],):
                c.start()
            dqacc[...] += dot_first(coefficient, keys)

    def over_y(d):
        @pl.when(has[d])
        def _():
            passed[d].wait_recv()
            ys[d] = (dkvs[d, 0].astype(F32) + cr[d].astype(F32)).astype(BF)
            for c in from_y[d]:
                c.start()

    dqacc[...] = jnp.zeros_like(dqacc)
    late = []
    for d in BACK:
        backward(d)
        if d != 2:
            late.append(d)
        if len(late) > 2:
            over_y(late.pop(0))
    for d in late:
        over_y(d)
    arrivals = []
    for e in (2, 1, 3):
        dqs[e - 1] = dqacc[pl.ds(e * ROWS, ROWS), :].astype(BF)
        arrivals.append(
            started(make(dqs.at[e - 1], dqr.at[e - 1], dsem.at[e - 1], drsem.at[e - 1], dev(dx=e)))
        )

    to_z = {}
    other = {o: zlo != o for o in (0, 1)}
    for d in BACK:
        to_z[d] = []
        for o in (0, 1):
            only = has[d] if d else other[o]
            c = make(
                zs.at[d, o], zr.at[d * 4 + zlo], asem.at[d * 2 + o], arsem.at[d * 4 + zlo],
                dev(dzhi=4 - d, dzlo=o + 4 - zlo), only,
            )
            to_z[d].append((c, only))

        @pl.when(has[d])
        def _():
            for c in from_y[d]:
                c.wait_recv()
            total = (dkvs[d, 0, :, mine, :] if d == 2 else ys[d, :, mine, :]).astype(F32)
            for i in range(1, 4):
                total = total + yr[d, i].astype(F32)
            if d == 2:
                for i in range(4):
                    total = total + yr[4, i].astype(F32)
            zs[d] = total.astype(BF)
            for c, only in to_z[d]:
                if d:
                    c.start()
                else:
                    pl.when(only)(c.start)

    for c in arrivals:
        c.wait_recv()
    query_grad = dqacc[pl.ds(0, ROWS), :]
    for e in range(3):
        query_grad = query_grad + dqr[e].astype(F32)
    out_ref[1] = query_grad.astype(BF)

    def arrived(c):
        pltpu.make_async_remote_copy(
            src_ref=zs.at[0, 0], dst_ref=c[0], send_sem=asem.at[0], recv_sem=c[1],
            device_id=dev(dcore=1), device_id_type=MESH,
        ).wait_recv()

    place = pl.ds(pl.multiple_of(y * 32, 32), 32)
    last = []
    for k in range(4):
        for f in (2, 1, 3, 0):
            only = owner if f else jnp.logical_and(owner, zlo != k)
            c = make(
                fin, out_ref.at[2 + zlo % 2, place, :], osem.at[k * 4 + f], orsem.at[f * 2 + zlo % 2],
                dev(dy=f, dzlo=k + 4 - zlo), only,
            )
            last.append((c, only))

    @pl.when(owner)
    def _():
        zr[zlo] = zs[0, zlo % 2]
        for k in range(4):

            @pl.when(zlo != k)
            def _():
                arrived((zr.at[k], arsem.at[k]))

        for d in (1, 3, 2):

            @pl.when(feeds[d])
            def _():
                for k in range(4):
                    arrived((zr.at[d * 4 + k], arsem.at[d * 4 + k]))

        total = zr[0].astype(F32)
        for i in range(1, 16):
            total = total + zr[i].astype(F32)
        fin[...] = total.astype(BF)
        for c, only in last:
            if only is owner:
                c.start()
            else:
                pl.when(only)(c.start)
        out_ref[2 + zlo % 2, place, :] = total.astype(BF)

    for o in (0, 1):
        for f in range(4):
            rows = pl.ds(pl.multiple_of(((y + 4 - f) % 4) * 32, 32), 32)
            wait = functools.partial(arrived, (out_ref.at[2 + o, rows, :], orsem.at[f * 2 + o]))
            if f:
                wait()
            else:
                pl.when(zlo != o)(wait)
    groups = []
    for c, only in sent:
        if only is None:
            c.wait_send()
        elif any(o is only for o, _ in groups):
            next(g for o, g in groups if o is only).append(c)
        else:
            groups.append((only, [c]))
    for only, group in groups:

        @pl.when(only)
        def _():
            for c in group:
                c.wait_send()


def local(query_rows, key_rows, value_rows, out_grad):
    dma = pltpu.SemaphoreType.DMA
    packed = pl.pallas_call(
        kernel,
        out_shape=jax.ShapeDtypeStruct((4, ROWS, D), BF),
        in_specs=[pl.BlockSpec(memory_space=pltpu.VMEM)],
        out_specs=pl.BlockSpec(memory_space=pltpu.VMEM),
        scratch_shapes=[
            pltpu.VMEM((4, ROWS, D), BF),
            pltpu.VMEM((4, ROWS, D), BF),
            pltpu.VMEM((ROWS, D), BF),
            pltpu.VMEM((4, 2, 2, ROWS, D), BF),
            pltpu.VMEM((4, 2 * ROWS, 4 * ROWS), F32),
            pltpu.VMEM((4, 2 * ROWS, 4 * ROWS), BF),
            pltpu.VMEM((4 * ROWS, D), F32),
            pltpu.VMEM((3, ROWS, D), BF),
            pltpu.VMEM((3, ROWS, D), BF),
            pltpu.VMEM((4 * ROWS, D), F32),
            pltpu.VMEM((3, ROWS, D), BF),
            pltpu.VMEM((3, ROWS, D), BF),
            pltpu.VMEM((4, 2, 2, ROWS, D), BF),
            pltpu.VMEM((4, 2, ROWS, D), BF),
            pltpu.VMEM((4, 2, ROWS, D), BF),
            pltpu.VMEM((5, 4, 2, 32, D), BF),
            pltpu.VMEM((4, 2, 32, D), BF),
            pltpu.VMEM((16, 32, D), BF),
            pltpu.VMEM((32, D), BF),
            dma((4,)), dma((3,)), dma((3,)), dma((6,)), dma((3,)), dma((3,)), dma((3, 4)), dma((3, 4)), dma((4,)), dma((4,)),
            dma((3,)), dma((3,)), dma((3,)), dma((3,)), dma((3,)), dma((3,)),
            dma((5, 4)), dma((5, 4)), dma((8,)), dma((16,)), dma((16,)), dma((8,)),
        ],
        compiler_params=pltpu.CompilerParams(
            collective_id=0, has_side_effects=True, vmem_limit_bytes=48 * 2**20
        ),
    )(jnp.stack((query_rows, key_rows, value_rows, out_grad)))
    return packed[0], packed[1], packed[2], packed[3]


def solution(mesh):
    return jax.shard_map(
        local,
        mesh=mesh,
        in_specs=(P("seq", "head"), P("seq", None), P("seq", None), P("seq", "head")),
        out_specs=(P("seq", "head"), P("seq", "head"), P("seq", None), P("seq", None)),
        check_vma=False,
    )
```
